768 devices in a mesh: dp: 12 (over z_lo, core), expert: 64 (over x, z_hi, y).
Axes of the slice: x: 4, y: 8, z: 12 (z_hi: 2, z_lo: 6; z = z_hi * 6 + z_lo), core: 2. Of those that a mesh axis runs over, the one named last changes fastest.
Arguments:
- tokens: bfloat16 [16384, 6144], P('expert', 'dp'), may hold values from -6 to 6
- grad_out: bfloat16 [16384, 6144], P('expert', 'dp'), may hold values from -6 to 6
- expert_ids: int32 [16384, 2], P('expert'), may hold values from 0 to 319, as said below
- gates: float32 [16384, 2], P('expert'), may hold values from 0.1 to 1
- w_in: bfloat16 [64, 6144, 2048], P('expert', 'dp'), may hold values from -0.078125 to 0.078125
- w_out: bfloat16 [64, 1024, 6144], P('expert', None, 'dp'), may hold values from -0.1875 to 0.1875
Outputs:
- moe_out: bfloat16 [16384, 6144], P('expert', 'dp')
- grad_tokens: bfloat16 [16384, 6144], P('expert', 'dp')
The draws below stay inside these ranges and needn't reach their ends.
Inputs may be any that keep to these rules, and one draw needn't show every extreme that they name: `expert_ids`: values of 64 or more name copy (identity) experts; every aligned block of 256 tokens holds exactly 128 entries under 64, and at most 3 of them name any one expert; in every draw one expert is named exactly 3 times in every block; a token's two entries may name the same expert.
All inputs are finite; a program needn't handle non-finite values.
Results may differ from the reference program's by a relative error of at most 0.017.
Values may be sent and summed in bfloat16 or wider, within the bound.
No kernel may reach another device: no remote copies, remote signals or barrier semaphores. Data moves between devices by JAX's collectives and lax.ppermute only.
A program may use at most 32 MiB of HBM per device.

```python
import jax
import jax.numpy as jnp
from jax import lax

MODEL_WIDTH = 6144
FF = 1024
ZEROS = 256
TOK_COL = 256
CAP = 3
ROUTED_EXPERTS = 64
REAL_DEV = 128
TOKENS = 16384
N_DP = 12
N_EXPERT = 64


def draw_expert_ids(key, part):
    base = jax.random.fold_in(key, 7)
    full_expert = jax.random.randint(jax.random.fold_in(base, 1), (), 0, ROUTED_EXPERTS)
    block_keys = jax.random.split(jax.random.fold_in(base, 2), N_EXPERT)
    count = ROUTED_EXPERTS * CAP

    def one_block(block_key):
        key_slots, key_entries, key_zeros = jax.random.split(block_key, 3)
        order = jax.random.permutation(key_slots, count).astype(jnp.int32)
        position = jnp.arange(count, dtype=jnp.int32)
        score = order - count * (position // CAP == full_expert).astype(jnp.int32)
        chosen = jnp.argsort(score, stable=True)[:REAL_DEV].astype(jnp.int32)
        entries = jax.random.permutation(key_entries, 2 * TOK_COL)[:REAL_DEV]
        names = ROUTED_EXPERTS + jax.random.randint(key_zeros, (2 * TOK_COL,), 0, ZEROS)
        return names.astype(jnp.int32).at[entries].set(chosen // CAP)
    names = jax.vmap(one_block)(block_keys)
    return names.reshape(N_EXPERT * TOK_COL, 2).astype(jnp.int32)


def level_of(own_key, shape, cuts, low, high):
    def one(dim, blocks):
        heights = jax.random.uniform(jax.random.fold_in(jax.random.fold_in(own_key, 6), dim), (blocks,), jnp.float32, low / len(cuts), high / len(cuts))
        return jnp.repeat(jnp.exp(heights), shape[dim] // blocks).reshape((-1,) + (1,) * (len(shape) - dim - 1))

    level = one(*cuts[0])
    for cut in cuts[1:]:
        level = level * one(*cut)
    return level


def noise(own_key, dims, scale, limit, cuts=(), kind=jnp.bfloat16):
    level = level_of(own_key, dims, cuts, -0.22, 0.18) if cuts else 1.0
    result = jax.random.normal(own_key, dims, jnp.float32) * scale * level
    return jnp.minimum(jnp.maximum(result, -limit), limit).astype(kind)


def setup_inputs(seed: int = 0) -> dict:
    splits = jax.random.split(jax.random.key(seed), 7)
    return {
        "tokens": noise(splits[0], (TOKENS, MODEL_WIDTH), 1.0, 6.0, ((0, 64), (1, 12))),
        "grad_out": noise(splits[1], (TOKENS, MODEL_WIDTH), 1.0, 6.0, ((0, 64), (1, 12))),
        "expert_ids": draw_expert_ids(jax.random.fold_in(splits[6], 71), 0),
        "gates": jnp.clip(0.1 + 0.9 * jax.random.uniform(splits[3], (TOKENS, 2), jnp.float32) ** level_of(splits[3], (TOKENS, 2), ((0, 64),), -0.2, 0.2), 0.1, 1.0),
        "w_in": noise(splits[4], (ROUTED_EXPERTS, MODEL_WIDTH, 2 * FF), MODEL_WIDTH ** -0.5, 0.078125, ((0, 64), (1, 12))),
        "w_out": noise(splits[5], (ROUTED_EXPERTS, FF, MODEL_WIDTH), FF ** -0.5, 0.1875, ((0, 64), (2, 12))),
    }


def finish(gate_up, hidden_grad, half):
    gate_part = gate_up[:, :half]
    up_part = gate_up[:, half:]
    sig = jax.nn.sigmoid(gate_part)
    silu = gate_part * sig
    dsilu = sig * (1.0 + gate_part * (1.0 - sig))
    hidden = (silu * up_part).astype(jnp.bfloat16)
    grads = jnp.concatenate([hidden_grad * up_part * dsilu, hidden_grad * silu], axis=1)
    return hidden, grads.astype(jnp.bfloat16)


def blocks_sum(partial_value):
    rounded = lax.optimization_barrier(partial_value.astype(jnp.bfloat16))
    return jnp.sum(rounded.astype(jnp.float32), axis=0)


def route_slots(expert_ids):
    flat = expert_ids.reshape(N_EXPERT, 2 * TOK_COL)
    onehot = (flat[:, :, None] == jnp.arange(ROUTED_EXPERTS, dtype=jnp.int32)[None, None, :]).astype(jnp.int32)
    before = jnp.cumsum(onehot, axis=1) - onehot
    return jnp.sum(before * onehot, axis=2).astype(jnp.int32).reshape(TOKENS, 2)


def reference(tokens, grad_out, expert_ids, gates, w_in, w_out):
    token_rows = N_EXPERT * CAP
    width = MODEL_WIDTH // N_DP
    half = FF
    slots = route_slots(expert_ids)
    source = (jnp.arange(TOKENS, dtype=jnp.int32) // TOK_COL)[:, None]
    real = expert_ids < ROUTED_EXPERTS
    target_position = jnp.where(real, expert_ids * token_rows + source * CAP + slots, ROUTED_EXPERTS * token_rows).astype(jnp.int32)
    xbuf = jnp.zeros((ROUTED_EXPERTS * token_rows, MODEL_WIDTH), jnp.bfloat16)
    gradient_buffer = jnp.zeros((ROUTED_EXPERTS * token_rows, MODEL_WIDTH), jnp.bfloat16)
    for expert_rank in range(2):
        xbuf = xbuf.at[target_position[:, expert_rank]].set(tokens, mode="drop")
        weighted_rows = (gates[:, expert_rank:expert_rank + 1] * grad_out.astype(jnp.float32)).astype(jnp.bfloat16)
        gradient_buffer = gradient_buffer.at[target_position[:, expert_rank]].set(weighted_rows, mode="drop")
    xbuf = xbuf.reshape(ROUTED_EXPERTS, token_rows, MODEL_WIDTH)
    gradient_buffer = gradient_buffer.reshape(ROUTED_EXPERTS, token_rows, MODEL_WIDTH)

    def per_expert(slot_index):
        x_rows = xbuf[slot_index]
        gradient_rows = gradient_buffer[slot_index]
        w_first = w_in[slot_index]
        w_second = w_out[slot_index]
        x_three = x_rows.astype(jnp.float32).reshape(token_rows, N_DP, width)
        g_three = gradient_rows.astype(jnp.float32).reshape(token_rows, N_DP, width)
        gate_up = blocks_sum(jnp.einsum("rnd,ndf->nrf", x_three, w_first.astype(jnp.float32).reshape(N_DP, width, 2 * FF)))
        hidden_grad = blocks_sum(jnp.einsum("rnd,fnd->nrf", g_three, w_second.astype(jnp.float32).reshape(half, N_DP, width)))
        hidden, gate_up_grad = finish(gate_up, hidden_grad, half)
        expert_out = jnp.dot(hidden, w_second, preferred_element_type=jnp.float32).astype(jnp.bfloat16)
        row_grad = jnp.dot(gate_up_grad, w_first.T, preferred_element_type=jnp.float32).astype(jnp.bfloat16)
        return expert_out, row_grad

    expert_out, row_grad = lax.map(per_expert, jnp.arange(ROUTED_EXPERTS, dtype=jnp.int32))
    out_flat = expert_out.reshape(ROUTED_EXPERTS * token_rows, MODEL_WIDTH)
    grad_flat = row_grad.reshape(ROUTED_EXPERTS * token_rows, MODEL_WIDTH)
    total_out = jnp.zeros((TOKENS, MODEL_WIDTH), jnp.float32)
    total_grad = jnp.zeros((TOKENS, MODEL_WIDTH), jnp.float32)
    for expert_rank in range(2):
        mask = real[:, expert_rank:expert_rank + 1]
        expert = jnp.where(real[:, expert_rank], expert_ids[:, expert_rank], 0).astype(jnp.int32)
        slot = jnp.where(real[:, expert_rank], slots[:, expert_rank], 0).astype(jnp.int32)
        first = (expert * token_rows + source[:, 0] * CAP + slot).astype(jnp.int32)
        pair_out = out_flat[first].astype(jnp.float32)
        pair_grad = grad_flat[first].astype(jnp.float32)
        weight = gates[:, expert_rank:expert_rank + 1]
        total_out = total_out + jnp.where(mask, weight * pair_out, weight * tokens.astype(jnp.float32))
        total_grad = total_grad + jnp.where(mask, pair_grad, weight * grad_out.astype(jnp.float32))
    return total_out.astype(jnp.bfloat16), total_grad.astype(jnp.bfloat16)
```

```python
import functools

import jax
import jax.numpy as jnp
from jax import lax
from jax.experimental import pallas as pl
from jax.experimental.pallas import tpu as pltpu
from jax.sharding import PartitionSpec as P

CAP = 3
LANES = 128
BF = jnp.bfloat16
F32 = jnp.float32
VMEM = pl.BlockSpec(memory_space=pltpu.VMEM)
SMEM = pl.BlockSpec(memory_space=pltpu.SMEM)


def call(body, outs, operands, scratch=(), flops=0):
    size = sum(o.size * o.dtype.itemsize for o in outs)
    size += sum(o.size * o.dtype.itemsize for o in operands)
    return pl.pallas_call(
        body,
        out_shape=list(outs),
        in_specs=[SMEM if o.ndim == 1 else VMEM for o in operands],
        out_specs=[VMEM] * len(outs),
        scratch_shapes=list(scratch),
        compiler_params=pltpu.CompilerParams(vmem_limit_bytes=32 * 1024 * 1024),
        cost_estimate=pl.CostEstimate(flops=flops, bytes_accessed=size, transcendentals=0),
    )(*operands)


def dot(a, b):
    return jnp.dot(a, b, preferred_element_type=F32)


def dot_t(a, b):
    return lax.dot_general(a, b, (((1,), (1,)), ((), ())), preferred_element_type=F32)


def pack(values, wide, n_dev):
    pieces = values[0].shape[1] // LANES
    stride = 2 * CAP * pieces
    for a, value in enumerate(values):
        for j in range(CAP):
            for q in range(pieces):
                place = (a * CAP + j) * pieces + q
                wide[pl.ds(place, n_dev, stride=stride), :] = value[
                    j * n_dev : (j + 1) * n_dev, q * LANES : (q + 1) * LANES
                ]


def unpack(wide, a, n_dev, width):
    pieces = width // LANES
    stride = 2 * CAP * pieces
    rows = []
    for j in range(CAP):
        columns = [
            wide[pl.ds((a * CAP + j) * pieces + q, n_dev, stride=stride), :] for q in range(pieces)
        ]
        rows.append(jnp.concatenate(columns, axis=1))
    return jnp.concatenate(rows, axis=0)


def send_body(n_dev, ids, gates, tokens, grad_out, send, picks, wide):
    t = tokens.shape[0]
    expert = lax.broadcasted_iota(jnp.int32, (n_dev, t), 0)
    hot = [jnp.where(expert == ids[k : k + 1, :], 1.0, 0.0) for k in range(2)]
    earlier = lax.broadcasted_iota(jnp.int32, (t, t), 0) < lax.broadcasted_iota(jnp.int32, (t, t), 1)
    before = dot((hot[0] + hot[1]).astype(BF), jnp.where(earlier, 1.0, 0.0).astype(BF))
    before = [before, before + hot[0]]
    picked = [
        jnp.concatenate(
            [jnp.where(before[k] == float(j), hot[k], 0.0) for j in range(CAP)], axis=0
        )
        for k in range(2)
    ]
    gate = jnp.sum(picked[0] * gates[0:1, :] + picked[1] * gates[1:2, :], axis=1, keepdims=True)
    both = (picked[0] + picked[1]).astype(BF)
    pack([dot(both, tokens[...]), dot(both, grad_out[...]) * gate], wide, n_dev)
    send[...] = wide[...].astype(BF)
    picks[...] = jnp.concatenate(picked, axis=1).astype(BF)


def first_body(n_dev, core, recv, w_in, w_out, partial, kept, wide, rows_x, rows_g):
    wide[...] = recv[...].astype(F32)
    width = w_in.shape[0]
    rows_x[...] = unpack(wide, 0, n_dev, width).astype(BF)
    rows_g[...] = unpack(wide, 1, n_dev, width).astype(BF)
    count = partial.shape[0]
    other = pl.ds(pl.multiple_of((1 - core[0]) * count, count), count)
    own = pl.ds(pl.multiple_of(core[0] * count, count), count)
    kept[:, :width] = rows_x[own, :]
    kept[:, width:] = rows_g[own, :]
    partial[:, : w_in.shape[1]] = dot(rows_x[other, :], w_in[...]).astype(BF)
    partial[:, w_in.shape[1] :] = dot_t(rows_g[other, :], w_out[...]).astype(BF)


def second_body(kept, w_in, w_out, partial):
    width = w_in.shape[0]
    partial[:, : w_in.shape[1]] = dot(kept[:, :width], w_in[...]).astype(BF)
    partial[:, w_in.shape[1] :] = dot_t(kept[:, width:], w_out[...]).astype(BF)


def own_body(hidden, w_in, w_out, rows):
    half, width = w_out.shape
    rows[:, :width] = dot(hidden[:, :half], w_out[...]).astype(BF)
    rows[:, width:] = dot_t(hidden[:, half:], w_in[...]).astype(BF)


def back_body(n_dev, core, hidden, own_rows, w_in, w_out, send, wide, rows):
    half, width = w_out.shape
    count = hidden.shape[0]
    other = pl.ds(pl.multiple_of((1 - core[0]) * count, count), count)
    own = pl.ds(pl.multiple_of(core[0] * count, count), count)
    rows[own, :] = own_rows[...].astype(F32)
    rows[other, :width] = dot(hidden[:, :half], w_out[...])
    rows[other, width:] = dot_t(hidden[:, half:], w_in[...])
    pack([rows[:, :width], rows[:, width:]], wide, n_dev)
    send[...] = wide[...].astype(BF)


def combine_body(n_dev, recv, picks, ids, gates, tokens, grad_out, moe_out, grad_tokens, wide):
    t, width = tokens.shape
    wide[...] = recv[...].astype(F32)
    back_out = unpack(wide, 0, n_dev, width).astype(BF)
    back_grad = unpack(wide, 1, n_dev, width).astype(BF)
    take = [picks[:, k * t : (k + 1) * t].astype(F32).T.astype(BF) for k in range(2)]
    copied = jnp.sum(jnp.where(ids[...] >= n_dev, gates[...], 0.0), axis=1, keepdims=True)
    moe = gates[:, 0:1] * dot(take[0], back_out) + gates[:, 1:2] * dot(take[1], back_out)
    moe_out[...] = (moe + copied * tokens[...].astype(F32)).astype(BF)
    grad = dot(take[0] + take[1], back_grad)
    grad_tokens[...] = (grad + copied * grad_out[...].astype(F32)).astype(BF)


def slice_of(array, start, count):
    return lax.dynamic_slice_in_dim(array, start, count, axis=0)


def per_device(tokens, grad_out, expert_ids, gates, w_in, w_out):
    n_dev = lax.axis_size("expert")
    n_dp = lax.axis_size("dp")
    t, width = tokens.shape
    half = w_out.shape[1]
    count = n_dev * CAP
    wide_rows = 2 * count * width // LANES
    w_first, w_second = w_in[0], w_out[0]
    wide = pltpu.VMEM((wide_rows, LANES), F32)
    shape = jax.ShapeDtypeStruct

    me = lax.axis_index("dp")
    core, pair, third = me % 2, (me // 2) % 2, me // 4
    cores = [(i, i ^ 1) for i in range(n_dp)]
    pairs = [(i, i ^ 2) for i in range(n_dp)]
    next_third = [(i, (i + 4) % n_dp) for i in range(n_dp)]
    last_third = [(i, (i + 8) % n_dp) for i in range(n_dp)]
    core_ref = core.astype(jnp.int32).reshape(1)

    send, picks = call(
        functools.partial(send_body, n_dev),
        [shape((wide_rows, LANES), BF), shape((count, 2 * t), BF)],
        [expert_ids.T, gates.T, tokens, grad_out],
        [wide],
        2 * (2 * count * t * width + n_dev * t * t),
    )

    def exchange(rows):
        parts = rows.reshape(n_dev, wide_rows // n_dev, LANES)
        parts = lax.all_to_all(parts, "expert", split_axis=0, concat_axis=0, tiled=True)
        return parts.reshape(wide_rows, LANES)

    recv = exchange(send)

    hidden_width = 3 * half
    n_core, n_pair, n_third = count // 2, count // 4, count // 12
    flops = 2 * n_core * width * hidden_width
    to_core, kept_rows = call(
        functools.partial(first_body, n_dev),
        [shape((n_core, hidden_width), BF), shape((n_core, 2 * width), BF)],
        [core_ref, recv, w_first, w_second],
        [wide, pltpu.VMEM((count, width), BF), pltpu.VMEM((count, width), BF)],
        flops,
    )
    from_core = lax.ppermute(to_core, "dp", cores)
    (mine,) = call(
        second_body, [shape((n_core, hidden_width), BF)], [kept_rows, w_first, w_second], [], flops
    )

    def two(start, rows):
        return slice_of(mine, start, rows).astype(F32) + slice_of(from_core, start, rows).astype(F32)

    from_pair = lax.ppermute(two((1 - pair) * n_pair, n_pair).astype(BF), "dp", pairs)

    def four(block):
        start = block * n_third
        return two(pair * n_pair + start, n_third) + slice_of(from_pair, start, n_third).astype(F32)

    after, before = (third + 1) % 3, (third + 2) % 3
    from_before = lax.ppermute(four(after).astype(BF), "dp", next_third)
    from_after = lax.ppermute(four(before).astype(BF), "dp", last_third)
    total = four(third) + from_before.astype(F32) + from_after.astype(F32)

    gate_part, up_part, hidden_grad = total[:, :half], total[:, half : 2 * half], total[:, 2 * half :]
    sig = jax.nn.sigmoid(gate_part)
    silu = gate_part * sig
    dsilu = sig * (1.0 + gate_part * (1.0 - sig))
    block = jnp.concatenate(
        [silu * up_part, hidden_grad * up_part * dsilu, hidden_grad * silu], axis=1
    ).astype(BF)

    of_before = lax.ppermute(block, "dp", next_third)
    of_after = lax.ppermute(block, "dp", last_third)
    ring = jnp.concatenate([block, of_after, of_before, block, of_after], axis=0)
    quarter = slice_of(ring, ((3 - third) % 3) * n_third, n_pair)
    other_quarter = lax.ppermute(quarter, "dp", pairs)
    own_half = jnp.concatenate(
        [
            jnp.where(pair == 0, quarter, other_quarter),
            jnp.where(pair == 0, other_quarter, quarter),
        ],
        axis=0,
    )
    other_half = lax.ppermute(own_half, "dp", cores)
    (own_rows,) = call(
        own_body, [shape((n_core, 2 * width), BF)], [own_half, w_first, w_second], [], flops
    )
    (send_back,) = call(
        functools.partial(back_body, n_dev),
        [shape((wide_rows, LANES), BF)],
        [core_ref, other_half, own_rows, w_first, w_second],
        [wide, pltpu.VMEM((count, 2 * width), F32)],
        flops,
    )
    recv_back = exchange(send_back)

    moe_out, grad_tokens = call(
        functools.partial(combine_body, n_dev),
        [shape((t, width), BF), shape((t, width), BF)],
        [recv_back, picks, expert_ids, gates, tokens, grad_out],
        [wide],
        2 * 3 * count * t * width,
    )
    return moe_out, grad_tokens


def solution(mesh):
    in_specs = (
        P("expert", "dp"),
        P("expert", "dp"),
        P("expert", None),
        P("expert", None),
        P("expert", "dp", None),
        P("expert", None, "dp"),
    )
    out_specs = (P("expert", "dp"), P("expert", "dp"))
    return jax.shard_map(
        per_device, mesh=mesh, in_specs=in_specs, out_specs=out_specs, check_vma=False
    )
```

```python
import functools

import jax
import jax.numpy as jnp
from jax import lax
from jax.experimental import pallas as pl
from jax.experimental.pallas import tpu as pltpu
from jax.sharding import PartitionSpec as P

CAP = 3
LANES = 128
CHUNKS = 1
BF = jnp.bfloat16
F32 = jnp.float32
VMEM = pl.BlockSpec(memory_space=pltpu.VMEM)
SMEM = pl.BlockSpec(memory_space=pltpu.SMEM)
HBM = pl.BlockSpec(memory_space=pltpu.HBM)


def call(body, outs, operands, scratch=(), flops=0, far=()):
    operands = [
        pltpu.with_memory_space_constraint(o, pltpu.HBM) if i in far else o
        for i, o in enumerate(operands)
    ]
    size = sum(o.size * o.dtype.itemsize for o in outs)
    size += sum(o.size * o.dtype.itemsize for o in operands)
    return pl.pallas_call(
        body,
        out_shape=list(outs),
        in_specs=[
            SMEM if o.ndim == 1 else HBM if i in far else VMEM for i, o in enumerate(operands)
        ],
        out_specs=[VMEM] * len(outs),
        scratch_shapes=list(scratch),
        compiler_params=pltpu.CompilerParams(vmem_limit_bytes=12 * 1024 * 1024),
        cost_estimate=pl.CostEstimate(flops=flops, bytes_accessed=size, transcendentals=0),
    )(*operands)


def dot(a, b):
    return jnp.dot(a, b, preferred_element_type=F32)


def dot_t(a, b):
    return lax.dot_general(a, b, (((1,), (1,)), ((), ())), preferred_element_type=F32)


def place_of(me):
    index = me[0]
    upper = jnp.where(index >= 6, 1, 0)
    return index & 1, upper, (index - 6 * upper) >> 1


def rows_at(start, count):
    return pl.ds(pl.multiple_of(start, 16), count)


def unpack(wide, a, n_dev, width):
    pieces = width // LANES
    stride = 2 * CAP * pieces
    rows = []
    for j in range(CAP):
        columns = [
            wide[pl.ds((a * CAP + j) * pieces + q, n_dev, stride=stride), :] for q in range(pieces)
        ]
        rows.append(jnp.concatenate(columns, axis=1))
    return jnp.concatenate(rows, axis=0)


def send_body(n_dev, ids_in, gates_in, tokens_in, grad_in, send, picks, ids, gates, tokens, grad, wide, sems):
    moves = [
        pltpu.make_async_copy(source, target, sems.at[i])
        for i, (source, target) in enumerate(
            [(ids_in, ids), (gates_in, gates), (tokens_in, tokens), (grad_in, grad)]
        )
    ]
    for move in moves:
        move.start()
    t, width = tokens.shape
    expert = lax.broadcasted_iota(jnp.int32, (n_dev, t), 0)
    earlier = lax.broadcasted_iota(jnp.int32, (t, t), 0) < lax.broadcasted_iota(jnp.int32, (t, t), 1)
    earlier = jnp.where(earlier, 1.0, 0.0).astype(BF)
    moves[0].wait()
    hot = [jnp.where(expert == ids[k : k + 1, :], 1.0, 0.0) for k in range(2)]
    before = dot((hot[0] + hot[1]).astype(BF), earlier)
    before = [before, before + hot[0]]
    picked = [
        jnp.concatenate(
            [jnp.where(before[k] == float(j), hot[k], 0.0) for j in range(CAP)], axis=0
        )
        for k in range(2)
    ]
    picks[...] = jnp.concatenate(picked, axis=1).astype(BF)
    both = (picked[0] + picked[1]).astype(BF)
    moves[1].wait()
    gate = jnp.sum(picked[0] * gates[0:1, :] + picked[1] * gates[1:2, :], axis=1, keepdims=True)
    pieces = width // LANES
    stride = 2 * CAP * pieces
    for a in range(2):
        moves[2 + a].wait()
        value = dot(both, tokens[...]) if a == 0 else dot(both, grad[...]) * gate
        for j in range(CAP):
            for q in range(pieces):
                wide[pl.ds((a * CAP + j) * pieces + q, n_dev, stride=stride), :] = value[
                    j * n_dev : (j + 1) * n_dev, q * LANES : (q + 1) * LANES
                ]
    send[...] = wide[...].astype(BF)


def product(out, rows_x, rows_g, w_in, w_out, chunk):
    half = w_out.shape[0]
    cut = half // CHUNKS
    a = chunk * cut
    out[:, :cut] = dot(rows_x, w_in[:, a : a + cut]).astype(BF)
    out[:, cut : 2 * cut] = dot(rows_x, w_in[:, half + a : half + a + cut]).astype(BF)
    out[:, 2 * cut :] = dot_t(rows_g, w_out[a : a + cut, :]).astype(BF)


def first_body(n_dev, me, recv, w_in_far, w_out_far, partial, rows, w_in, w_out, wide, sems):
    moves = [
        pltpu.make_async_copy(w_in_far, w_in, sems.at[0]),
        pltpu.make_async_copy(w_out_far, w_out, sems.at[1]),
    ]
    for move in moves:
        move.start()
    wide[...] = recv[...].astype(F32)
    width = w_in.shape[0]
    for a in range(2):
        rows[:, a * width : (a + 1) * width] = unpack(wide, a, n_dev, width).astype(BF)
    count = partial.shape[0]
    other = rows_at((1 - place_of(me)[0]) * count, count)
    for move in moves:
        move.wait()
    product(partial, rows[other, :width], rows[other, width:], w_in, w_out, 0)


def part_body(own, chunk, me, rows, w_in, w_out, partial):
    width = w_in.shape[0]
    count = partial.shape[0]
    core = place_of(me)[0]
    part = rows_at((core if own else 1 - core) * count, count)
    product(partial, rows[part, :width], rows[part, width:], w_in, w_out, chunk)


def third_body(me, mine, from_core, to_after, to_before, total):
    chip = place_of(me)[2]
    count = total.shape[0]

    def two(block):
        block = jnp.where(block >= 3, block - 3, block)
        part = rows_at(block * count, count)
        return mine[part, :].astype(F32) + from_core[part, :].astype(F32)

    to_after[...] = two(chip + 1).astype(BF)
    to_before[...] = two(chip + 2).astype(BF)
    total[...] = two(chip)


def half_body(total, from_before, from_after, to_half, total_out):
    value = total[...] + from_before[...].astype(F32) + from_after[...].astype(F32)
    to_half[...] = value.astype(BF)
    total_out[...] = value


def finish_body(total, from_half, block):
    cut = total.shape[1] // 3
    value = total[...] + from_half[...].astype(F32)
    gate_part, up_part, hidden_grad = value[:, :cut], value[:, cut : 2 * cut], value[:, 2 * cut :]
    sig = jax.nn.sigmoid(gate_part)
    silu = gate_part * sig
    dsilu = sig * (1.0 + gate_part * (1.0 - sig))
    block[:, :cut] = (silu * up_part).astype(BF)
    block[:, cut : 2 * cut] = (hidden_grad * up_part * dsilu).astype(BF)
    block[:, 2 * cut :] = (hidden_grad * silu).astype(BF)


def join_body(*refs):
    out = refs[-1]
    count = refs[0].shape[0]
    for i, ref in enumerate(refs[:-1]):
        out[i * count : (i + 1) * count, :] = ref[...]


def expert_rows(hidden, w_in, w_out, chunk):
    half = w_out.shape[0]
    cut = half // CHUNKS
    a = chunk * cut
    value = dot(hidden[:, :cut], w_out[a : a + cut, :])
    grad = dot_t(hidden[:, cut : 2 * cut], w_in[:, a : a + cut])
    grad = grad + dot_t(hidden[:, 2 * cut :], w_in[:, half + a : half + a + cut])
    return value, grad


def rows_body(chunk, hidden, w_in, w_out, *rest):
    out = rest[-1]
    width = w_in.shape[0]
    value, grad = expert_rows(hidden, w_in, w_out, chunk)
    if chunk:
        value, grad = rest[0][:, :width] + value, rest[0][:, width:] + grad
    out[:, :width] = value
    out[:, width:] = grad


def back_body(n_dev, me, hidden, own_rows, w_in, w_out, *rest):
    send, wide = rest[-2:]
    width = w_in.shape[0]
    value, grad = expert_rows(hidden, w_in, w_out, CHUNKS - 1)
    if CHUNKS > 1:
        value, grad = rest[0][:, :width] + value, rest[0][:, width:] + grad
    core, _, chip = place_of(me)
    pieces = width // LANES
    stride = 2 * CAP * pieces
    count = hidden.shape[0] // 6
    for c in range(2):
        for i in range(6):
            block = chip + i // 2
            block = jnp.where(block >= 3, block - 3, block)
            row = ((core ^ c) * 6 + block * 2 + i % 2) * count
            slot = row // n_dev
            start = (row - slot * n_dev) * stride + slot * pieces
            for a in range(2):
                for q in range(pieces):
                    left = q * LANES
                    if c == 0:
                        left = left + a * width
                        piece = own_rows[i * count : (i + 1) * count, left : left + LANES]
                    else:
                        piece = (value, grad)[a][i * count : (i + 1) * count, left : left + LANES]
                    at = pl.ds(start + a * CAP * pieces + q, count, stride=stride)
                    wide[at, :] = piece
    send[...] = wide[...].astype(BF)


def combine_body(n_dev, recv, picks, ids, gates, tokens, grad_out, moe_out, grad_tokens, wide):
    t, width = tokens.shape
    wide[...] = recv[...].astype(F32)
    back_out = unpack(wide, 0, n_dev, width).astype(BF)
    back_grad = unpack(wide, 1, n_dev, width).astype(BF)
    take = [picks[:, k * t : (k + 1) * t].astype(F32).T.astype(BF) for k in range(2)]
    copied = jnp.sum(jnp.where(ids[...] >= n_dev, gates[...], 0.0), axis=1, keepdims=True)
    moe = gates[:, 0:1] * dot(take[0], back_out) + gates[:, 1:2] * dot(take[1], back_out)
    moe_out[...] = (moe + copied * tokens[...].astype(F32)).astype(BF)
    grad = dot(take[0] + take[1], back_grad)
    grad_tokens[...] = (grad + copied * grad_out[...].astype(F32)).astype(BF)


def per_device(tokens, grad_out, expert_ids, gates, w_in, w_out):
    n_dev = lax.axis_size("expert")
    n_dp = lax.axis_size("dp")
    t, width = tokens.shape
    half = w_out.shape[1]
    count = n_dev * CAP
    wide_rows = 2 * count * width // LANES
    weights = (w_in[0], w_out[0])
    wide = pltpu.VMEM((wide_rows, LANES), F32)
    shape = jax.ShapeDtypeStruct

    me = lax.axis_index("dp").astype(jnp.int32).reshape(1)
    cores = [(i, i ^ 1) for i in range(n_dp)]
    halves = [(i, (i + 6) % n_dp) for i in range(n_dp)]
    after = [(i, i // 6 * 6 + (i + 2) % 6) for i in range(n_dp)]
    before = [(i, i // 6 * 6 + (i + 4) % 6) for i in range(n_dp)]

    send, picks = call(
        functools.partial(send_body, n_dev),
        [shape((wide_rows, LANES), BF), shape((count, 2 * t), BF)],
        [expert_ids.T, gates.T, tokens, grad_out],
        [
            pltpu.VMEM((2, t), jnp.int32),
            pltpu.VMEM((2, t), F32),
            pltpu.VMEM((t, width), BF),
            pltpu.VMEM((t, width), BF),
            wide,
            pltpu.SemaphoreType.DMA((4,)),
        ],
        2 * (2 * count * t * width + n_dev * t * t),
        range(4),
    )

    def exchange(rows):
        parts = rows.reshape(n_dev, wide_rows // n_dev, LANES)
        parts = lax.all_to_all(parts, "expert", split_axis=0, concat_axis=0, tiled=True)
        return parts.reshape(wide_rows, LANES)

    recv = exchange(send)

    cw = 3 * half // CHUNKS
    n_core, n_third = count // 2, count // 6
    flops = 2 * n_core * width * cw
    chunks = range(CHUNKS)
    to_core, rows = call(
        functools.partial(first_body, n_dev),
        [shape((n_core, cw), BF), shape((count, 2 * width), BF)],
        [me, recv, *weights],
        [
            pltpu.VMEM(weights[0].shape, BF),
            pltpu.VMEM(weights[1].shape, BF),
            wide,
            pltpu.SemaphoreType.DMA((2,)),
        ],
        flops,
        (2, 3),
    )

    def part(own, chunk):
        body = functools.partial(part_body, own, chunk)
        return call(body, [shape((n_core, cw), BF)], [me, rows, *weights], (), flops)[0]

    to_core = [to_core] + [part(False, h) for h in chunks[1:]]
    from_core = [lax.ppermute(to_core[h], "dp", cores) for h in chunks]
    mine = [part(True, h) for h in chunks]
    blocks = []
    for h in chunks:
        to_after, to_before, total = call(
            third_body,
            [shape((n_third, cw), BF), shape((n_third, cw), BF), shape((n_third, cw), F32)],
            [me, mine[h], from_core[h]],
        )
        from_before = lax.ppermute(to_after, "dp", after)
        from_after = lax.ppermute(to_before, "dp", before)
        to_half, total = call(
            half_body,
            [shape((n_third, cw), BF), shape((n_third, cw), F32)],
            [total, from_before, from_after],
        )
        from_half = lax.ppermute(to_half, "dp", halves)
        blocks.append(call(finish_body, [shape((n_third, cw), BF)], [total, from_half])[0])
    own_half, other_half = [], []
    for h in chunks:
        of_before = lax.ppermute(blocks[h], "dp", after)
        of_after = lax.ppermute(blocks[h], "dp", before)
        own_half.append(
            call(join_body, [shape((n_core, cw), BF)], [blocks[h], of_after, of_before])[0]
        )
        other_half.append(lax.ppermute(own_half[h], "dp", cores))

    def expert(hidden, upto):
        so_far = []
        for h in range(upto):
            so_far = call(
                functools.partial(rows_body, h),
                [shape((n_core, 2 * width), F32)],
                [hidden[h], *weights, *so_far],
                (),
                flops,
            )
        return so_far

    (send_back,) = call(
        functools.partial(back_body, n_dev),
        [shape((wide_rows, LANES), BF)],
        [me, other_half[-1], *expert(own_half, CHUNKS), *weights, *expert(other_half, CHUNKS - 1)],
        [wide],
        flops,
    )
    recv_back = exchange(send_back)

    moe_out, grad_tokens = call(
        functools.partial(combine_body, n_dev),
        [shape((t, width), BF), shape((t, width), BF)],
        [recv_back, picks, expert_ids, gates, tokens, grad_out],
        [wide],
        2 * 3 * count * t * width,
    )
    return moe_out, grad_tokens


def solution(mesh):
    in_specs = (
        P("expert", "dp"),
        P("expert", "dp"),
        P("expert", None),
        P("expert", None),
        P("expert", "dp", None),
        P("expert", None, "dp"),
    )
    out_specs = (P("expert", "dp"), P("expert", "dp"))
    return jax.shard_map(
        per_device, mesh=mesh, in_specs=in_specs, out_specs=out_specs, check_vma=False
    )
```

```python
import functools

import jax
import jax.numpy as jnp
from jax import lax
from jax.experimental import pallas as pl
from jax.experimental.pallas import tpu as pltpu
from jax.sharding import PartitionSpec as P

CAP = 3
LANES = 128
CHUNKS = 1
BF = jnp.bfloat16
F32 = jnp.float32
VMEM = pl.BlockSpec(memory_space=pltpu.VMEM)
SMEM = pl.BlockSpec(memory_space=pltpu.SMEM)
HBM = pl.BlockSpec(memory_space=pltpu.HBM)


def call(body, outs, operands, scratch=(), flops=0, far=()):
    out_far = [i for i, o in enumerate(outs) if not isinstance(o, jax.ShapeDtypeStruct)]
    operands = [
        pltpu.with_memory_space_constraint(o, pltpu.HBM) if i in far else o
        for i, o in enumerate(operands)
    ]
    size = sum(o.size * o.dtype.itemsize for o in operands)
    return pl.pallas_call(
        body,
        out_shape=list(outs),
        in_specs=[
            SMEM if o.ndim == 1 else HBM if i in far else VMEM for i, o in enumerate(operands)
        ],
        out_specs=[HBM if i in out_far else VMEM for i in range(len(outs))],
        scratch_shapes=list(scratch),
        compiler_params=pltpu.CompilerParams(vmem_limit_bytes=12 * 1024 * 1024),
        cost_estimate=pl.CostEstimate(flops=flops, bytes_accessed=size, transcendentals=0),
    )(*operands)


def dot(a, b):
    return jnp.dot(a, b, preferred_element_type=F32)


def dot_t(a, b):
    return lax.dot_general(a, b, (((1,), (1,)), ((), ())), preferred_element_type=F32)


def place_of(me):
    index = me[0]
    upper = jnp.where(index >= 6, 1, 0)
    return index & 1, upper, (index - 6 * upper) >> 1


def rows_at(start, count):
    return pl.ds(pl.multiple_of(start, 16), count)


def unpack(wide, a, n_dev, width):
    pieces = width // LANES
    stride = 2 * CAP * pieces
    rows = []
    for j in range(CAP):
        columns = [
            wide[pl.ds((a * CAP + j) * pieces + q, n_dev, stride=stride), :] for q in range(pieces)
        ]
        rows.append(jnp.concatenate(columns, axis=1))
    return jnp.concatenate(rows, axis=0)


def started(sources, targets, sems):
    moves = [
        pltpu.make_async_copy(source, target, sems.at[i])
        for i, (source, target) in enumerate(zip(sources, targets))
    ]
    for move in moves:
        move.start()
    return moves


def send_body(n_dev, *refs):
    send_out, picks_out, weigh_out, w_in, w_out, *rest = refs[6:]
    send, picks, weigh, ids, gates, tokens, grad, wide, sems, out_sems = rest
    moves = started(refs[:6], (ids, gates, tokens, grad, w_in, w_out), sems)
    t, width = tokens.shape
    expert = lax.broadcasted_iota(jnp.int32, (n_dev, t), 0)
    earlier = lax.broadcasted_iota(jnp.int32, (t, t), 0) < lax.broadcasted_iota(jnp.int32, (t, t), 1)
    earlier = jnp.where(earlier, 1.0, 0.0).astype(BF)
    moves[0].wait()
    hot = [jnp.where(expert == ids[k : k + 1, :], 1.0, 0.0) for k in range(2)]
    before = dot((hot[0] + hot[1]).astype(BF), earlier)
    before = [before, before + hot[0]]
    picked = [
        jnp.concatenate(
            [jnp.where(before[k] == float(j), hot[k], 0.0) for j in range(CAP)], axis=0
        )
        for k in range(2)
    ]
    picks[...] = jnp.concatenate(picked, axis=1).astype(BF)
    outs = started((picks,), (picks_out,), out_sems)
    both = (picked[0] + picked[1]).astype(BF)
    moves[1].wait()
    gate = jnp.sum(picked[0] * gates[0:1, :] + picked[1] * gates[1:2, :], axis=1, keepdims=True)
    copied = jnp.sum(jnp.where(ids[...] >= n_dev, gates[...], 0.0), axis=0, keepdims=True)
    lines = [gates[...], copied, jnp.zeros((5, t), F32)]
    weigh[...] = jnp.concatenate(lines, axis=0).T
    outs += started((weigh,), (weigh_out,), out_sems.at[pl.ds(1, 1)])
    pieces = width // LANES
    stride = 2 * CAP * pieces
    for a in range(2):
        moves[2 + a].wait()
        value = dot(both, tokens[...]) if a == 0 else dot(both, grad[...]) * gate
        for j in range(CAP):
            for q in range(pieces):
                wide[pl.ds((a * CAP + j) * pieces + q, n_dev, stride=stride), :] = value[
                    j * n_dev : (j + 1) * n_dev, q * LANES : (q + 1) * LANES
                ]
    part = wide.shape[0] // 4
    for i in range(4):
        rows = pl.ds(i * part, part)
        send[rows, :] = wide[rows, :].astype(BF)
        outs += started((send.at[rows],), (send_out.at[rows],), out_sems.at[pl.ds(2 + i, 1)])
    for move in moves[4:] + outs:
        move.wait()


def product(out, rows_x, rows_g, w_in, w_out, chunk):
    half = w_out.shape[0]
    cut = half // CHUNKS
    a = chunk * cut
    out[:, :cut] = dot(rows_x, w_in[:, a : a + cut]).astype(BF)
    out[:, cut : 2 * cut] = dot(rows_x, w_in[:, half + a : half + a + cut]).astype(BF)
    out[:, 2 * cut :] = dot_t(rows_g, w_out[a : a + cut, :]).astype(BF)


def first_body(n_dev, me, recv, w_in, w_out, partial, rows, wide):
    wide[...] = recv[...].astype(F32)
    width = w_in.shape[0]
    for a in range(2):
        rows[:, a * width : (a + 1) * width] = unpack(wide, a, n_dev, width).astype(BF)
    count = partial.shape[0]
    other = rows_at((1 - place_of(me)[0]) * count, count)
    product(partial, rows[other, :width], rows[other, width:], w_in, w_out, 0)


def part_body(own, chunk, me, rows, w_in, w_out, partial):
    width = w_in.shape[0]
    count = partial.shape[0]
    core = place_of(me)[0]
    part = rows_at((core if own else 1 - core) * count, count)
    product(partial, rows[part, :width], rows[part, width:], w_in, w_out, chunk)


def third_body(me, mine, from_core, to_after, to_before, total):
    chip = place_of(me)[2]
    count = total.shape[0]

    def two(block):
        block = jnp.where(block >= 3, block - 3, block)
        part = rows_at(block * count, count)
        return mine[part, :].astype(F32) + from_core[part, :].astype(F32)

    to_after[...] = two(chip + 1).astype(BF)
    to_before[...] = two(chip + 2).astype(BF)
    total[...] = two(chip)


def half_body(total, from_before, from_after, to_half, total_out):
    value = total[...] + from_before[...].astype(F32) + from_after[...].astype(F32)
    to_half[...] = value.astype(BF)
    total_out[...] = value


def finish_body(total, from_half, block):
    cut = total.shape[1] // 3
    value = total[...] + from_half[...].astype(F32)
    gate_part, up_part, hidden_grad = value[:, :cut], value[:, cut : 2 * cut], value[:, 2 * cut :]
    sig = jax.nn.sigmoid(gate_part)
    silu = gate_part * sig
    dsilu = sig * (1.0 + gate_part * (1.0 - sig))
    block[:, :cut] = (silu * up_part).astype(BF)
    block[:, cut : 2 * cut] = (hidden_grad * up_part * dsilu).astype(BF)
    block[:, 2 * cut :] = (hidden_grad * silu).astype(BF)


def join_body(*refs):
    out = refs[-1]
    count = refs[0].shape[0]
    for i, ref in enumerate(refs[:-1]):
        out[i * count : (i + 1) * count, :] = ref[...]


def expert_rows(hidden, w_in, w_out, chunk):
    half = w_out.shape[0]
    cut = half // CHUNKS
    a = chunk * cut
    value = dot(hidden[:, :cut], w_out[a : a + cut, :])
    grad = dot_t(hidden[:, cut : 2 * cut], w_in[:, a : a + cut])
    grad = grad + dot_t(hidden[:, 2 * cut :], w_in[:, half + a : half + a + cut])
    return value, grad


def rows_body(chunk, hidden, w_in, w_out, *rest):
    out = rest[-1]
    width = w_in.shape[0]
    value, grad = expert_rows(hidden, w_in, w_out, chunk)
    if chunk:
        value, grad = rest[0][:, :width] + value, rest[0][:, width:] + grad
    out[:, :width] = value
    out[:, width:] = grad


def back_body(n_dev, me, hidden, own_rows, w_in, w_out, *rest):
    send, wide = rest[-2:]
    width = w_in.shape[0]
    value, grad = expert_rows(hidden, w_in, w_out, CHUNKS - 1)
    if CHUNKS > 1:
        value, grad = rest[0][:, :width] + value, rest[0][:, width:] + grad
    core, _, chip = place_of(me)
    pieces = width // LANES
    stride = 2 * CAP * pieces
    count = hidden.shape[0] // 6
    for c in range(2):
        for i in range(6):
            block = chip + i // 2
            block = jnp.where(block >= 3, block - 3, block)
            row = ((core ^ c) * 6 + block * 2 + i % 2) * count
            slot = row // n_dev
            start = (row - slot * n_dev) * stride + slot * pieces
            for a in range(2):
                for q in range(pieces):
                    left = q * LANES
                    if c == 0:
                        left = left + a * width
                        piece = own_rows[i * count : (i + 1) * count, left : left + LANES]
                    else:
                        piece = (value, grad)[a][i * count : (i + 1) * count, left : left + LANES]
                    at = pl.ds(start + a * CAP * pieces + q, count, stride=stride)
                    wide[at, :] = piece
    send[...] = wide[...].astype(BF)


def combine_body(n_dev, recv, picks, weigh, *refs):
    moe_out, grad_tokens, tokens, grad_out, wide, sems = refs[2:]
    moves = started(refs[:2], (tokens, grad_out), sems)
    t, width = tokens.shape
    wide[...] = recv[...].astype(F32)
    back_out = unpack(wide, 0, n_dev, width).astype(BF)
    back_grad = unpack(wide, 1, n_dev, width).astype(BF)
    take = [picks[:, k * t : (k + 1) * t].astype(F32).T.astype(BF) for k in range(2)]
    copied = weigh[:, 2:3]
    moe = weigh[:, 0:1] * dot(take[0], back_out) + weigh[:, 1:2] * dot(take[1], back_out)
    moves[0].wait()
    moe_out[...] = (moe + copied * tokens[...].astype(F32)).astype(BF)
    grad = dot(take[0] + take[1], back_grad)
    moves[1].wait()
    grad_tokens[...] = (grad + copied * grad_out[...].astype(F32)).astype(BF)


def per_device(tokens, grad_out, expert_ids, gates, w_in, w_out):
    n_dev = lax.axis_size("expert")
    n_dp = lax.axis_size("dp")
    t, width = tokens.shape
    half = w_out.shape[1]
    count = n_dev * CAP
    wide_rows = 2 * count * width // LANES
    wide = pltpu.VMEM((wide_rows, LANES), F32)
    shape = jax.ShapeDtypeStruct

    me = lax.axis_index("dp").astype(jnp.int32).reshape(1)
    cores = [(i, i ^ 1) for i in range(n_dp)]
    halves = [(i, (i + 6) % n_dp) for i in range(n_dp)]
    after = [(i, i // 6 * 6 + (i + 2) % 6) for i in range(n_dp)]
    before = [(i, i // 6 * 6 + (i + 4) % 6) for i in range(n_dp)]

    send, picks, weigh, *weights = call(
        functools.partial(send_body, n_dev),
        [
            pltpu.HBM((wide_rows, LANES), BF),
            pltpu.HBM((count, 2 * t), BF),
            pltpu.HBM((t, 8), F32),
            shape(w_in.shape[1:], BF),
            shape(w_out.shape[1:], BF),
        ],
        [expert_ids.T, gates.T, tokens, grad_out, w_in[0], w_out[0]],
        [
            pltpu.VMEM((wide_rows, LANES), BF),
            pltpu.VMEM((count, 2 * t), BF),
            pltpu.VMEM((t, 8), F32),
            pltpu.VMEM((2, t), jnp.int32),
            pltpu.VMEM((2, t), F32),
            pltpu.VMEM((t, width), BF),
            pltpu.VMEM((t, width), BF),
            wide,
            pltpu.SemaphoreType.DMA((6,)),
            pltpu.SemaphoreType.DMA((6,)),
        ],
        2 * (2 * count * t * width + n_dev * t * t),
        range(6),
    )

    def exchange(rows):
        parts = rows.reshape(n_dev, wide_rows // n_dev, LANES)
        parts = lax.all_to_all(parts, "expert", split_axis=0, concat_axis=0, tiled=True)
        return parts.reshape(wide_rows, LANES)

    recv = exchange(send)

    cw = 3 * half // CHUNKS
    n_core, n_third = count // 2, count // 6
    flops = 2 * n_core * width * cw
    chunks = range(CHUNKS)
    to_core, rows = call(
        functools.partial(first_body, n_dev),
        [shape((n_core, cw), BF), shape((count, 2 * width), BF)],
        [me, recv, *weights],
        [wide],
        flops,
    )

    def part(own, chunk):
        body = functools.partial(part_body, own, chunk)
        return call(body, [shape((n_core, cw), BF)], [me, rows, *weights], (), flops)[0]

    to_core = [to_core] + [part(False, h) for h in chunks[1:]]
    from_core = [lax.ppermute(to_core[h], "dp", cores) for h in chunks]
    mine = [part(True, h) for h in chunks]
    blocks = []
    for h in chunks:
        to_after, to_before, total = call(
            third_body,
            [shape((n_third, cw), BF), shape((n_third, cw), BF), shape((n_third, cw), F32)],
            [me, mine[h], from_core[h]],
        )
        from_before = lax.ppermute(to_after, "dp", after)
        from_after = lax.ppermute(to_before, "dp", before)
        to_half, total = call(
            half_body,
            [shape((n_third, cw), BF), shape((n_third, cw), F32)],
            [total, from_before, from_after],
        )
        from_half = lax.ppermute(to_half, "dp", halves)
        blocks.append(call(finish_body, [shape((n_third, cw), BF)], [total, from_half])[0])
    own_half, other_half = [], []
    for h in chunks:
        of_before = lax.ppermute(blocks[h], "dp", after)
        of_after = lax.ppermute(blocks[h], "dp", before)
        own_half.append(
            call(join_body, [shape((n_core, cw), BF)], [blocks[h], of_after, of_before])[0]
        )
        other_half.append(lax.ppermute(own_half[h], "dp", cores))

    def expert(hidden, upto):
        so_far = []
        for h in range(upto):
            so_far = call(
                functools.partial(rows_body, h),
                [shape((n_core, 2 * width), F32)],
                [hidden[h], *weights, *so_far],
                (),
                flops,
            )
        return so_far

    (send_back,) = call(
        functools.partial(back_body, n_dev),
        [shape((wide_rows, LANES), BF)],
        [me, other_half[-1], *expert(own_half, CHUNKS), *weights, *expert(other_half, CHUNKS - 1)],
        [wide],
        flops,
    )
    recv_back = exchange(send_back)

    moe_out, grad_tokens = call(
        functools.partial(combine_body, n_dev),
        [shape((t, width), BF), shape((t, width), BF)],
        [recv_back, picks, weigh, tokens, grad_out],
        [
            pltpu.VMEM((t, width), BF),
            pltpu.VMEM((t, width), BF),
            wide,
            pltpu.SemaphoreType.DMA((2,)),
        ],
        2 * 3 * count * t * width,
        (3, 4),
    )
    return moe_out, grad_tokens


def solution(mesh):
    in_specs = (
        P("expert", "dp"),
        P("expert", "dp"),
        P("expert", None),
        P("expert", None),
        P("expert", "dp", None),
        P("expert", None, "dp"),
    )
    out_specs = (P("expert", "dp"), P("expert", "dp"))
    return jax.shard_map(
        per_device, mesh=mesh, in_specs=in_specs, out_specs=out_specs, check_vma=False
    )
```

```python
import functools

import jax
import jax.numpy as jnp
from jax import lax
from jax.experimental import pallas as pl
from jax.experimental.pallas import tpu as pltpu
from jax.sharding import PartitionSpec as P

CAP = 3
LANES = 128
CHUNKS = 1
BF = jnp.bfloat16
F32 = jnp.float32
VMEM = pl.BlockSpec(memory_space=pltpu.VMEM)
SMEM = pl.BlockSpec(memory_space=pltpu.SMEM)
HBM = pl.BlockSpec(memory_space=pltpu.HBM)


def call(body, outs, operands, scratch=(), flops=0, far=()):
    out_far = [i for i, o in enumerate(outs) if not isinstance(o, jax.ShapeDtypeStruct)]
    operands = [
        pltpu.with_memory_space_constraint(o, pltpu.HBM) if i in far else o
        for i, o in enumerate(operands)
    ]
    size = sum(o.size * o.dtype.itemsize for o in operands)
    return pl.pallas_call(
        body,
        out_shape=list(outs),
        in_specs=[
            SMEM if o.ndim == 1 else HBM if i in far else VMEM for i, o in enumerate(operands)
        ],
        out_specs=[HBM if i in out_far else VMEM for i in range(len(outs))],
        scratch_shapes=list(scratch),
        compiler_params=pltpu.CompilerParams(vmem_limit_bytes=12 * 1024 * 1024),
        cost_estimate=pl.CostEstimate(flops=flops, bytes_accessed=size, transcendentals=0),
    )(*operands)


def dot(a, b):
    return jnp.dot(a, b, preferred_element_type=F32)


def dot_t(a, b):
    return lax.dot_general(a, b, (((1,), (1,)), ((), ())), preferred_element_type=F32)


def place_of(me):
    index = me[0]
    upper = jnp.where(index >= 6, 1, 0)
    return index & 1, upper, (index - 6 * upper) >> 1


def rows_at(start, count):
    return pl.ds(pl.multiple_of(start, 16), count)


def unpack(wide, a, n_dev, width):
    pieces = width // LANES
    stride = 2 * CAP * pieces
    rows = []
    for j in range(CAP):
        columns = [
            wide[pl.ds((a * CAP + j) * pieces + q, n_dev, stride=stride), :] for q in range(pieces)
        ]
        rows.append(jnp.concatenate(columns, axis=1))
    return jnp.concatenate(rows, axis=0)


def started(sources, targets, sems):
    moves = [
        pltpu.make_async_copy(source, target, sems.at[i])
        for i, (source, target) in enumerate(zip(sources, targets))
    ]
    for move in moves:
        move.start()
    return moves


def send_body(n_dev, *refs):
    send_out, picks_out, weigh_out, w_in, w_out, *rest = refs[6:]
    send, picks, weigh, ids, gates, tokens, grad, wide, sems, out_sems = rest
    moves = started(refs[:6], (ids, gates, tokens, grad, w_in, w_out), sems)
    t, width = tokens.shape
    expert = lax.broadcasted_iota(jnp.int32, (n_dev, t), 0)
    earlier = lax.broadcasted_iota(jnp.int32, (t, t), 0) < lax.broadcasted_iota(jnp.int32, (t, t), 1)
    earlier = jnp.where(earlier, 1.0, 0.0).astype(BF)
    moves[0].wait()
    hot = [jnp.where(expert == ids[k : k + 1, :], 1.0, 0.0) for k in range(2)]
    before = dot((hot[0] + hot[1]).astype(BF), earlier)
    before = [before, before + hot[0]]
    picked = [
        jnp.concatenate(
            [jnp.where(before[k] == float(j), hot[k], 0.0) for j in range(CAP)], axis=0
        )
        for k in range(2)
    ]
    for k in range(2):
        picks[:, k * CAP * n_dev : (k + 1) * CAP * n_dev] = picked[k].T.astype(BF)
    outs = started((picks,), (picks_out,), out_sems)
    both = (picked[0] + picked[1]).astype(BF)
    moves[1].wait()
    gate = jnp.sum(picked[0] * gates[0:1, :] + picked[1] * gates[1:2, :], axis=1, keepdims=True)
    copied = jnp.sum(jnp.where(ids[...] >= n_dev, gates[...], 0.0), axis=0, keepdims=True)
    lines = [gates[...], copied, jnp.zeros((5, t), F32)]
    weigh[...] = jnp.concatenate(lines, axis=0).T
    outs += started((weigh,), (weigh_out,), out_sems.at[pl.ds(1, 1)])
    pieces = width // LANES
    stride = 2 * CAP * pieces
    for a in range(2):
        moves[2 + a].wait()
        value = dot(both, tokens[...]) if a == 0 else dot(both, grad[...]) * gate
        for j in range(CAP):
            for q in range(pieces):
                wide[pl.ds((a * CAP + j) * pieces + q, n_dev, stride=stride), :] = value[
                    j * n_dev : (j + 1) * n_dev, q * LANES : (q + 1) * LANES
                ]
    part = wide.shape[0] // 4
    for i in range(4):
        rows = pl.ds(i * part, part)
        send[rows, :] = wide[rows, :].astype(BF)
        outs += started((send.at[rows],), (send_out.at[rows],), out_sems.at[pl.ds(2 + i, 1)])
    for move in moves[4:] + outs:
        move.wait()


def product(out, rows_x, rows_g, w_in, w_out, chunk):
    half = w_out.shape[0]
    cut = half // CHUNKS
    a = chunk * cut
    out[:, :cut] = dot(rows_x, w_in[:, a : a + cut]).astype(BF)
    out[:, cut : 2 * cut] = dot(rows_x, w_in[:, half + a : half + a + cut]).astype(BF)
    out[:, 2 * cut :] = dot_t(rows_g, w_out[a : a + cut, :]).astype(BF)


def first_body(n_dev, me, recv, w_in, w_out, partial, rows, wide):
    wide[...] = recv[...].astype(F32)
    width = w_in.shape[0]
    for a in range(2):
        rows[:, a * width : (a + 1) * width] = unpack(wide, a, n_dev, width).astype(BF)
    count = partial.shape[0]
    other = rows_at((1 - place_of(me)[0]) * count, count)
    product(partial, rows[other, :width], rows[other, width:], w_in, w_out, 0)


def part_body(own, chunk, me, rows, w_in, w_out, partial):
    width = w_in.shape[0]
    count = partial.shape[0]
    core = place_of(me)[0]
    part = rows_at((core if own else 1 - core) * count, count)
    product(partial, rows[part, :width], rows[part, width:], w_in, w_out, chunk)


def third_body(me, mine, from_core, to_after, to_before, total):
    chip = place_of(me)[2]
    count = total.shape[0]

    def two(block):
        block = jnp.where(block >= 3, block - 3, block)
        part = rows_at(block * count, count)
        return mine[part, :].astype(F32) + from_core[part, :].astype(F32)

    to_after[...] = two(chip + 1).astype(BF)
    to_before[...] = two(chip + 2).astype(BF)
    total[...] = two(chip)


def half_body(total, from_before, from_after, to_half, total_out):
    value = total[...] + from_before[...].astype(F32) + from_after[...].astype(F32)
    to_half[...] = value.astype(BF)
    total_out[...] = value


def finish_body(total, from_half, block):
    cut = total.shape[1] // 3
    value = total[...] + from_half[...].astype(F32)
    gate_part, up_part, hidden_grad = value[:, :cut], value[:, cut : 2 * cut], value[:, 2 * cut :]
    sig = jax.nn.sigmoid(gate_part)
    silu = gate_part * sig
    dsilu = sig * (1.0 + gate_part * (1.0 - sig))
    block[:, :cut] = (silu * up_part).astype(BF)
    block[:, cut : 2 * cut] = (hidden_grad * up_part * dsilu).astype(BF)
    block[:, 2 * cut :] = (hidden_grad * silu).astype(BF)


def join_body(*refs):
    out = refs[-1]
    count = refs[0].shape[0]
    for i, ref in enumerate(refs[:-1]):
        out[i * count : (i + 1) * count, :] = ref[...]


def expert_rows(hidden, w_in, w_out, chunk):
    half = w_out.shape[0]
    cut = half // CHUNKS
    a = chunk * cut
    value = dot(hidden[:, :cut], w_out[a : a + cut, :])
    grad = dot_t(hidden[:, cut : 2 * cut], w_in[:, a : a + cut])
    grad = grad + dot_t(hidden[:, 2 * cut :], w_in[:, half + a : half + a + cut])
    return value, grad


def rows_body(hidden, w_in, w_out, tokens_in, grad_in, out, tokens, grad_out, sems):
    moves = started((tokens_in, grad_in), (tokens, grad_out), sems)
    width = w_in.shape[0]
    value, grad = expert_rows(hidden, w_in, w_out, 0)
    out[:, :width] = value
    out[:, width:] = grad
    for move in moves:
        move.wait()


def back_body(n_dev, me, hidden, own_rows, w_in, w_out, *rest):
    send, wide = rest[-2:]
    width = w_in.shape[0]
    value, grad = expert_rows(hidden, w_in, w_out, CHUNKS - 1)
    if CHUNKS > 1:
        value, grad = rest[0][:, :width] + value, rest[0][:, width:] + grad
    core, _, chip = place_of(me)
    pieces = width // LANES
    stride = 2 * CAP * pieces
    count = hidden.shape[0] // 6
    for c in range(2):
        for i in range(6):
            block = chip + i // 2
            block = jnp.where(block >= 3, block - 3, block)
            row = ((core ^ c) * 6 + block * 2 + i % 2) * count
            slot = row // n_dev
            start = (row - slot * n_dev) * stride + slot * pieces
            for a in range(2):
                for q in range(pieces):
                    left = q * LANES
                    if c == 0:
                        left = left + a * width
                        piece = own_rows[i * count : (i + 1) * count, left : left + LANES]
                    else:
                        piece = (value, grad)[a][i * count : (i + 1) * count, left : left + LANES]
                    at = pl.ds(start + a * CAP * pieces + q, count, stride=stride)
                    wide[at, :] = piece
    send[...] = wide[...].astype(BF)


def combine_body(n_dev, recv, picks, weigh, tokens, grad_out, moe_out, grad_tokens, wide):
    t, width = tokens.shape
    wide[...] = recv[...].astype(F32)
    back_out = unpack(wide, 0, n_dev, width).astype(BF)
    back_grad = unpack(wide, 1, n_dev, width).astype(BF)
    count = CAP * n_dev
    take = [picks[:, :count], picks[:, count:]]
    copied = weigh[:, 2:3]
    moe = weigh[:, 0:1] * dot(take[0], back_out) + weigh[:, 1:2] * dot(take[1], back_out)
    moe_out[...] = (moe + copied * tokens[...].astype(F32)).astype(BF)
    grad = dot(take[0] + take[1], back_grad)
    grad_tokens[...] = (grad + copied * grad_out[...].astype(F32)).astype(BF)


def per_device(tokens, grad_out, expert_ids, gates, w_in, w_out):
    n_dev = lax.axis_size("expert")
    n_dp = lax.axis_size("dp")
    t, width = tokens.shape
    half = w_out.shape[1]
    count = n_dev * CAP
    wide_rows = 2 * count * width // LANES
    wide = pltpu.VMEM((wide_rows, LANES), F32)
    shape = jax.ShapeDtypeStruct

    me = lax.axis_index("dp").astype(jnp.int32).reshape(1)
    cores = [(i, i ^ 1) for i in range(n_dp)]
    halves = [(i, (i + 6) % n_dp) for i in range(n_dp)]
    after = [(i, i // 6 * 6 + (i + 2) % 6) for i in range(n_dp)]
    before = [(i, i // 6 * 6 + (i + 4) % 6) for i in range(n_dp)]

    send, picks, weigh, *weights = call(
        functools.partial(send_body, n_dev),
        [
            pltpu.HBM((wide_rows, LANES), BF),
            pltpu.HBM((t, 2 * count), BF),
            pltpu.HBM((t, 8), F32),
            shape(w_in.shape[1:], BF),
            shape(w_out.shape[1:], BF),
        ],
        [expert_ids.T, gates.T, tokens, grad_out, w_in[0], w_out[0]],
        [
            pltpu.VMEM((wide_rows, LANES), BF),
            pltpu.VMEM((t, 2 * count), BF),
            pltpu.VMEM((t, 8), F32),
            pltpu.VMEM((2, t), jnp.int32),
            pltpu.VMEM((2, t), F32),
            pltpu.VMEM((t, width), BF),
            pltpu.VMEM((t, width), BF),
            wide,
            pltpu.SemaphoreType.DMA((6,)),
            pltpu.SemaphoreType.DMA((6,)),
        ],
        2 * (2 * count * t * width + n_dev * t * t),
        range(6),
    )

    def exchange(rows):
        parts = rows.reshape(n_dev, wide_rows // n_dev, LANES)
        parts = lax.all_to_all(parts, "expert", split_axis=0, concat_axis=0, tiled=True)
        return parts.reshape(wide_rows, LANES)

    recv = exchange(send)

    cw = 3 * half // CHUNKS
    n_core, n_third = count // 2, count // 6
    flops = 2 * n_core * width * cw
    chunks = range(CHUNKS)
    to_core, rows = call(
        functools.partial(first_body, n_dev),
        [shape((n_core, cw), BF), shape((count, 2 * width), BF)],
        [me, recv, *weights],
        [wide],
        flops,
    )

    def part(own, chunk):
        body = functools.partial(part_body, own, chunk)
        return call(body, [shape((n_core, cw), BF)], [me, rows, *weights], (), flops)[0]

    to_core = [to_core] + [part(False, h) for h in chunks[1:]]
    from_core = [lax.ppermute(to_core[h], "dp", cores) for h in chunks]
    mine = [part(True, h) for h in chunks]
    blocks = []
    for h in chunks:
        to_after, to_before, total = call(
            third_body,
            [shape((n_third, cw), BF), shape((n_third, cw), BF), shape((n_third, cw), F32)],
            [me, mine[h], from_core[h]],
        )
        from_before = lax.ppermute(to_after, "dp", after)
        from_after = lax.ppermute(to_before, "dp", before)
        to_half, total = call(
            half_body,
            [shape((n_third, cw), BF), shape((n_third, cw), F32)],
            [total, from_before, from_after],
        )
        from_half = lax.ppermute(to_half, "dp", halves)
        blocks.append(call(finish_body, [shape((n_third, cw), BF)], [total, from_half])[0])
    own_half, other_half = [], []
    for h in chunks:
        of_before = lax.ppermute(blocks[h], "dp", after)
        of_after = lax.ppermute(blocks[h], "dp", before)
        own_half.append(
            call(join_body, [shape((n_core, cw), BF)], [blocks[h], of_after, of_before])[0]
        )
        other_half.append(lax.ppermute(own_half[h], "dp", cores))

    own_rows, tokens, grad_out = call(
        rows_body,
        [shape((n_core, 2 * width), F32), shape((t, width), BF), shape((t, width), BF)],
        [own_half[0], *weights, tokens, grad_out],
        [pltpu.SemaphoreType.DMA((2,))],
        flops,
        (3, 4),
    )

    (send_back,) = call(
        functools.partial(back_body, n_dev),
        [shape((wide_rows, LANES), BF)],
        [me, other_half[0], own_rows, *weights],
        [wide],
        flops,
    )
    recv_back = exchange(send_back)

    moe_out, grad_tokens = call(
        functools.partial(combine_body, n_dev),
        [shape((t, width), BF), shape((t, width), BF)],
        [recv_back, picks, weigh, tokens, grad_out],
        [wide],
        2 * 3 * count * t * width,
    )
    return moe_out, grad_tokens


def solution(mesh):
    in_specs = (
        P("expert", "dp"),
        P("expert", "dp"),
        P("expert", None),
        P("expert", None),
        P("expert", "dp", None),
        P("expert", None, "dp"),
    )
    out_specs = (P("expert", "dp"), P("expert", "dp"))
    return jax.shard_map(
        per_device, mesh=mesh, in_specs=in_specs, out_specs=out_specs, check_vma=False
    )
```

```python
import functools

import jax
import jax.numpy as jnp
from jax import lax
from jax.experimental import pallas as pl
from jax.experimental.pallas import tpu as pltpu
from jax.sharding import PartitionSpec as P

CAP = 3
LANES = 128
BF = jnp.bfloat16
F32 = jnp.float32
VMEM = pl.BlockSpec(memory_space=pltpu.VMEM)
SMEM = pl.BlockSpec(memory_space=pltpu.SMEM)
HBM = pl.BlockSpec(memory_space=pltpu.HBM)


def call(body, outs, operands, scratch=(), flops=0, far=()):
    out_far = [i for i, o in enumerate(outs) if not isinstance(o, jax.ShapeDtypeStruct)]
    operands = [
        pltpu.with_memory_space_constraint(o, pltpu.HBM) if i in far else o
        for i, o in enumerate(operands)
    ]
    size = sum(o.size * o.dtype.itemsize for o in operands)
    return pl.pallas_call(
        body,
        out_shape=list(outs),
        in_specs=[
            SMEM if o.ndim == 1 else HBM if i in far else VMEM for i, o in enumerate(operands)
        ],
        out_specs=[HBM if i in out_far else VMEM for i in range(len(outs))],
        scratch_shapes=list(scratch),
        compiler_params=pltpu.CompilerParams(vmem_limit_bytes=12 * 1024 * 1024),
        cost_estimate=pl.CostEstimate(flops=flops, bytes_accessed=size, transcendentals=0),
    )(*operands)


def dot(a, b):
    return jnp.dot(a, b, preferred_element_type=F32)


def dot_t(a, b):
    return lax.dot_general(a, b, (((1,), (1,)), ((), ())), preferred_element_type=F32)


def place_of(me):
    index = me[0]
    upper = jnp.where(index >= 6, 1, 0)
    return index & 1, upper, (index - 6 * upper) >> 1


def rows_at(start, count):
    return pl.ds(pl.multiple_of(start, 16), count)


def unpack(wide, a, n_dev, width):
    pieces = width // LANES
    stride = 2 * CAP * pieces
    rows = []
    for j in range(CAP):
        columns = [
            wide[pl.ds((a * CAP + j) * pieces + q, n_dev, stride=stride), :] for q in range(pieces)
        ]
        rows.append(jnp.concatenate(columns, axis=1))
    return jnp.concatenate(rows, axis=0)


def started(sources, targets, sems):
    moves = [
        pltpu.make_async_copy(source, target, sems.at[i])
        for i, (source, target) in enumerate(zip(sources, targets))
    ]
    for move in moves:
        move.start()
    return moves


def one_hot(n_dev, ids):
    t = ids.shape[1]
    expert = lax.broadcasted_iota(jnp.int32, (n_dev, t), 0)
    hot = [jnp.where(expert == ids[k : k + 1, :], 1.0, 0.0) for k in range(2)]
    earlier = lax.broadcasted_iota(jnp.int32, (t, t), 0) < lax.broadcasted_iota(jnp.int32, (t, t), 1)
    before = dot((hot[0] + hot[1]).astype(BF), jnp.where(earlier, 1.0, 0.0).astype(BF))
    before = [before, before + hot[0]]
    return [
        jnp.concatenate(
            [jnp.where(before[k] == float(j), hot[k], 0.0) for j in range(CAP)], axis=0
        )
        for k in range(2)
    ]


def send_body(n_dev, *refs):
    send_out, ids, gates, tokens, grad, send, wide, sems, out_sems = refs[4:]
    moves = started(refs[:4], (ids, gates, tokens, grad), sems)
    width = tokens.shape[1]
    moves[0].wait()
    picked = one_hot(n_dev, ids)
    both = (picked[0] + picked[1]).astype(BF)
    moves[1].wait()
    gate = jnp.sum(picked[0] * gates[0:1, :] + picked[1] * gates[1:2, :], axis=1, keepdims=True)
    pieces = width // LANES
    stride = 2 * CAP * pieces
    for a in range(2):
        moves[2 + a].wait()
        value = dot(both, tokens[...]) if a == 0 else dot(both, grad[...]) * gate
        for j in range(CAP):
            for q in range(pieces):
                wide[pl.ds((a * CAP + j) * pieces + q, n_dev, stride=stride), :] = value[
                    j * n_dev : (j + 1) * n_dev, q * LANES : (q + 1) * LANES
                ]
    part = wide.shape[0] // 4
    outs = []
    for i in range(4):
        rows = pl.ds(i * part, part)
        send[rows, :] = wide[rows, :].astype(BF)
        outs += started((send.at[rows],), (send_out.at[rows],), out_sems.at[pl.ds(i, 1)])
    for move in outs:
        move.wait()


def ready_body(n_dev, *refs):
    picks_out, weigh_out, w_in, w_out, picks, weigh, ids, gates, sems, out_sems = refs[4:]
    moves = started(refs[:4], (ids, gates, w_in, w_out), sems)
    t = ids.shape[1]
    moves[0].wait()
    count = CAP * n_dev
    for k, picked in enumerate(one_hot(n_dev, ids)):
        picks[:, k * count : (k + 1) * count] = picked.T.astype(BF)
    outs = started((picks,), (picks_out,), out_sems)
    moves[1].wait()
    copied = jnp.sum(jnp.where(ids[...] >= n_dev, gates[...], 0.0), axis=0, keepdims=True)
    weigh[...] = jnp.concatenate([gates[...], copied, jnp.zeros((5, t), F32)], axis=0).T
    outs += started((weigh,), (weigh_out,), out_sems.at[pl.ds(1, 1)])
    for move in moves[2:] + outs:
        move.wait()


def product(out, rows_x, rows_g, w_in, w_out):
    cut = w_in.shape[1]
    out[:, :cut] = dot(rows_x, w_in[...]).astype(BF)
    out[:, cut:] = dot_t(rows_g, w_out[...]).astype(BF)


def first_body(n_dev, me, recv, w_in, w_out, partial, rows, wide):
    wide[...] = recv[...].astype(F32)
    width = w_in.shape[0]
    for a in range(2):
        rows[:, a * width : (a + 1) * width] = unpack(wide, a, n_dev, width).astype(BF)
    count = partial.shape[0]
    other = rows_at((1 - place_of(me)[0]) * count, count)
    product(partial, rows[other, :width], rows[other, width:], w_in, w_out)


def own_body(me, rows, w_in, w_out, partial):
    width = w_in.shape[0]
    count = partial.shape[0]
    own = rows_at(place_of(me)[0] * count, count)
    product(partial, rows[own, :width], rows[own, width:], w_in, w_out)


def third_body(me, mine, from_core, to_after, to_before, total):
    chip = place_of(me)[2]
    count = total.shape[0]

    def two(block):
        block = jnp.where(block >= 3, block - 3, block)
        part = rows_at(block * count, count)
        return mine[part, :].astype(F32) + from_core[part, :].astype(F32)

    to_after[...] = two(chip + 1).astype(BF)
    to_before[...] = two(chip + 2).astype(BF)
    total[...] = two(chip)


def half_body(total, from_before, from_after, to_half, total_out):
    value = total[...] + from_before[...].astype(F32) + from_after[...].astype(F32)
    to_half[...] = value.astype(BF)
    total_out[...] = value


def finish_body(total, from_half, block):
    cut = total.shape[1] // 3
    value = total[...] + from_half[...].astype(F32)
    gate_part, up_part, hidden_grad = value[:, :cut], value[:, cut : 2 * cut], value[:, 2 * cut :]
    sig = jax.nn.sigmoid(gate_part)
    silu = gate_part * sig
    dsilu = sig * (1.0 + gate_part * (1.0 - sig))
    block[:, :cut] = (silu * up_part).astype(BF)
    block[:, cut : 2 * cut] = (hidden_grad * up_part * dsilu).astype(BF)
    block[:, 2 * cut :] = (hidden_grad * silu).astype(BF)


def join_body(*refs):
    out = refs[-1]
    count = refs[0].shape[0]
    for i, ref in enumerate(refs[:-1]):
        out[i * count : (i + 1) * count, :] = ref[...]


def expert_rows(hidden, w_in, w_out):
    half = w_out.shape[0]
    return dot(hidden[:, :half], w_out[...]), dot_t(hidden[:, half:], w_in[...])


def rows_body(hidden, w_in, w_out, tokens_in, grad_in, out, tokens, grad_out, sems):
    moves = started((tokens_in, grad_in), (tokens, grad_out), sems)
    width = w_in.shape[0]
    value, grad = expert_rows(hidden, w_in, w_out)
    out[:, :width] = value
    out[:, width:] = grad
    for move in moves:
        move.wait()


def back_body(n_dev, me, hidden, own_rows, w_in, w_out, send, wide):
    width = w_in.shape[0]
    value, grad = expert_rows(hidden, w_in, w_out)
    core, _, chip = place_of(me)
    pieces = width // LANES
    stride = 2 * CAP * pieces
    count = hidden.shape[0] // 6
    for c in range(2):
        for i in range(6):
            block = chip + i // 2
            block = jnp.where(block >= 3, block - 3, block)
            row = ((core ^ c) * 6 + block * 2 + i % 2) * count
            slot = row // n_dev
            start = (row - slot * n_dev) * stride + slot * pieces
            for a in range(2):
                for q in range(pieces):
                    left = q * LANES
                    if c == 0:
                        left = left + a * width
                        piece = own_rows[i * count : (i + 1) * count, left : left + LANES]
                    else:
                        piece = (value, grad)[a][i * count : (i + 1) * count, left : left + LANES]
                    at = pl.ds(start + a * CAP * pieces + q, count, stride=stride)
                    wide[at, :] = piece
    send[...] = wide[...].astype(BF)


def combine_body(n_dev, recv, picks, weigh, tokens, grad_out, moe_out, grad_tokens, wide):
    t, width = tokens.shape
    wide[...] = recv[...].astype(F32)
    back_out = unpack(wide, 0, n_dev, width).astype(BF)
    back_grad = unpack(wide, 1, n_dev, width).astype(BF)
    count = CAP * n_dev
    take = [picks[:, :count], picks[:, count:]]
    copied = weigh[:, 2:3]
    moe = weigh[:, 0:1] * dot(take[0], back_out) + weigh[:, 1:2] * dot(take[1], back_out)
    moe_out[...] = (moe + copied * tokens[...].astype(F32)).astype(BF)
    grad = dot(take[0] + take[1], back_grad)
    grad_tokens[...] = (grad + copied * grad_out[...].astype(F32)).astype(BF)


def per_device(tokens, grad_out, expert_ids, gates, w_in, w_out):
    n_dev = lax.axis_size("expert")
    n_dp = lax.axis_size("dp")
    t, width = tokens.shape
    half = w_out.shape[1]
    count = n_dev * CAP
    wide_rows = 2 * count * width // LANES
    wide = pltpu.VMEM((wide_rows, LANES), F32)
    shape = jax.ShapeDtypeStruct

    me = lax.axis_index("dp").astype(jnp.int32).reshape(1)
    cores = [(i, i ^ 1) for i in range(n_dp)]
    halves = [(i, (i + 6) % n_dp) for i in range(n_dp)]
    after = [(i, i // 6 * 6 + (i + 2) % 6) for i in range(n_dp)]
    before = [(i, i // 6 * 6 + (i + 4) % 6) for i in range(n_dp)]

    lines = [pltpu.VMEM((2, t), jnp.int32), pltpu.VMEM((2, t), F32)]
    (send,) = call(
        functools.partial(send_body, n_dev),
        [pltpu.HBM((wide_rows, LANES), BF)],
        [expert_ids.T, gates.T, tokens, grad_out],
        [
            *lines,
            pltpu.VMEM((t, width), BF),
            pltpu.VMEM((t, width), BF),
            pltpu.VMEM((wide_rows, LANES), BF),
            wide,
            pltpu.SemaphoreType.DMA((4,)),
            pltpu.SemaphoreType.DMA((4,)),
        ],
        2 * (2 * count * t * width + n_dev * t * t),
        range(4),
    )
    picks, weigh, *weights = call(
        functools.partial(ready_body, n_dev),
        [
            pltpu.HBM((t, 2 * count), BF),
            pltpu.HBM((t, 8), F32),
            shape(w_in.shape[1:], BF),
            shape(w_out.shape[1:], BF),
        ],
        [expert_ids.T, gates.T, w_in[0], w_out[0]],
        [
            pltpu.VMEM((t, 2 * count), BF),
            pltpu.VMEM((t, 8), F32),
            *lines,
            pltpu.SemaphoreType.DMA((4,)),
            pltpu.SemaphoreType.DMA((2,)),
        ],
        2 * n_dev * t * t,
        range(4),
    )

    def exchange(rows):
        parts = rows.reshape(n_dev, wide_rows // n_dev, LANES)
        parts = lax.all_to_all(parts, "expert", split_axis=0, concat_axis=0, tiled=True)
        return parts.reshape(wide_rows, LANES)

    recv = exchange(send)

    cw = 3 * half
    n_core, n_third = count // 2, count // 6
    flops = 2 * n_core * width * cw
    to_core, rows = call(
        functools.partial(first_body, n_dev),
        [shape((n_core, cw), BF), shape((count, 2 * width), BF)],
        [me, recv, *weights],
        [wide],
        flops,
    )
    from_core = lax.ppermute(to_core, "dp", cores)
    (mine,) = call(own_body, [shape((n_core, cw), BF)], [me, rows, *weights], (), flops)

    third = shape((n_third, cw), BF)
    wide_third = shape((n_third, cw), F32)
    to_after, to_before, total = call(third_body, [third, third, wide_third], [me, mine, from_core])
    from_before = lax.ppermute(to_after, "dp", after)
    from_after = lax.ppermute(to_before, "dp", before)
    to_half, total = call(half_body, [third, wide_third], [total, from_before, from_after])
    from_half = lax.ppermute(to_half, "dp", halves)
    (block,) = call(finish_body, [third], [total, from_half])
    of_before = lax.ppermute(block, "dp", after)
    of_after = lax.ppermute(block, "dp", before)
    (own_half,) = call(join_body, [shape((n_core, cw), BF)], [block, of_after, of_before])
    other_half = lax.ppermute(own_half, "dp", cores)

    own_rows, tokens, grad_out = call(
        rows_body,
        [shape((n_core, 2 * width), F32), shape((t, width), BF), shape((t, width), BF)],
        [own_half, *weights, tokens, grad_out],
        [pltpu.SemaphoreType.DMA((2,))],
        flops,
        (3, 4),
    )

    (send_back,) = call(
        functools.partial(back_body, n_dev),
        [shape((wide_rows, LANES), BF)],
        [me, other_half, own_rows, *weights],
        [wide],
        flops,
    )
    recv_back = exchange(send_back)

    moe_out, grad_tokens = call(
        functools.partial(combine_body, n_dev),
        [shape((t, width), BF), shape((t, width), BF)],
        [recv_back, picks, weigh, tokens, grad_out],
        [wide],
        2 * 3 * count * t * width,
    )
    return moe_out, grad_tokens


def solution(mesh):
    in_specs = (
        P("expert", "dp"),
        P("expert", "dp"),
        P("expert", None),
        P("expert", None),
        P("expert", "dp", None),
        P("expert", None, "dp"),
    )
    out_specs = (P("expert", "dp"), P("expert", "dp"))
    return jax.shard_map(
        per_device, mesh=mesh, in_specs=in_specs, out_specs=out_specs, check_vma=False
    )
```

```python
import functools

import jax
import jax.numpy as jnp
from jax import lax
from jax.experimental import pallas as pl
from jax.experimental.pallas import tpu as pltpu
from jax.sharding import PartitionSpec as P

CAP = 3
LANES = 128
BF = jnp.bfloat16
F32 = jnp.float32
VMEM = pl.BlockSpec(memory_space=pltpu.VMEM)
SMEM = pl.BlockSpec(memory_space=pltpu.SMEM)
HBM = pl.BlockSpec(memory_space=pltpu.HBM)


def call(body, outs, operands, scratch=(), flops=0, far=()):
    out_far = [i for i, o in enumerate(outs) if not isinstance(o, jax.ShapeDtypeStruct)]
    operands = [
        pltpu.with_memory_space_constraint(o, pltpu.HBM) if i in far else o
        for i, o in enumerate(operands)
    ]
    size = sum(o.size * o.dtype.itemsize for o in operands)
    return pl.pallas_call(
        body,
        out_shape=list(outs),
        in_specs=[
            SMEM if o.ndim == 1 else HBM if i in far else VMEM for i, o in enumerate(operands)
        ],
        out_specs=[HBM if i in out_far else VMEM for i in range(len(outs))],
        scratch_shapes=list(scratch),
        compiler_params=pltpu.CompilerParams(vmem_limit_bytes=12 * 1024 * 1024),
        cost_estimate=pl.CostEstimate(flops=flops, bytes_accessed=size, transcendentals=0),
    )(*operands)


def dot(a, b):
    return jnp.dot(a, b, preferred_element_type=F32)


def dot_t(a, b):
    return lax.dot_general(a, b, (((1,), (1,)), ((), ())), preferred_element_type=F32)


def place_of(me):
    index = me[0]
    upper = jnp.where(index >= 6, 1, 0)
    return index & 1, upper, (index - 6 * upper) >> 1


def rows_at(start, count):
    return pl.ds(pl.multiple_of(start, 16), count)


def unpack(wide, a, n_dev, width):
    pieces = width // LANES
    stride = 2 * CAP * pieces
    rows = []
    for j in range(CAP):
        columns = [
            wide[pl.ds((a * CAP + j) * pieces + q, n_dev, stride=stride), :] for q in range(pieces)
        ]
        rows.append(jnp.concatenate(columns, axis=1))
    return jnp.concatenate(rows, axis=0)


def started(sources, targets, sems):
    moves = [
        pltpu.make_async_copy(source, target, sems.at[i])
        for i, (source, target) in enumerate(zip(sources, targets))
    ]
    for move in moves:
        move.start()
    return moves


def one_hot(n_dev, ids):
    t = ids.shape[1]
    expert = lax.broadcasted_iota(jnp.int32, (n_dev, t), 0)
    hot = [jnp.where(expert == ids[k : k + 1, :], 1.0, 0.0) for k in range(2)]
    earlier = lax.broadcasted_iota(jnp.int32, (t, t), 0) < lax.broadcasted_iota(jnp.int32, (t, t), 1)
    before = dot((hot[0] + hot[1]).astype(BF), jnp.where(earlier, 1.0, 0.0).astype(BF))
    before = [before, before + hot[0]]
    return [
        jnp.concatenate(
            [jnp.where(before[k] == float(j), hot[k], 0.0) for j in range(CAP)], axis=0
        )
        for k in range(2)
    ]


def send_body(n_dev, *refs):
    send_out, ids, gates, tokens, grad, send, wide, sems, out_sems = refs[4:]
    moves = started(refs[:4], (ids, gates, tokens, grad), sems)
    width = tokens.shape[1]
    moves[0].wait()
    picked = one_hot(n_dev, ids)
    both = (picked[0] + picked[1]).astype(BF)
    moves[1].wait()
    gate = jnp.sum(picked[0] * gates[0:1, :] + picked[1] * gates[1:2, :], axis=1, keepdims=True)
    pieces = width // LANES
    stride = 2 * CAP * pieces
    for a in range(2):
        moves[2 + a].wait()
        value = dot(both, tokens[...]) if a == 0 else dot(both, grad[...]) * gate
        for j in range(CAP):
            for q in range(pieces):
                wide[pl.ds((a * CAP + j) * pieces + q, n_dev, stride=stride), :] = value[
                    j * n_dev : (j + 1) * n_dev, q * LANES : (q + 1) * LANES
                ]
    part = wide.shape[0] // 4
    outs = []
    for i in range(4):
        rows = pl.ds(i * part, part)
        send[rows, :] = wide[rows, :].astype(BF)
        outs += started((send.at[rows],), (send_out.at[rows],), out_sems.at[pl.ds(i, 1)])
    for move in outs:
        move.wait()


def ready_body(n_dev, *refs):
    picks_out, weigh_out, w_in, w_out, picks, weigh, ids, gates, sems, out_sems = refs[4:]
    moves = started(refs[:4], (ids, gates, w_in, w_out), sems)
    t = ids.shape[1]
    moves[0].wait()
    count = CAP * n_dev
    for k, picked in enumerate(one_hot(n_dev, ids)):
        picks[:, k * count : (k + 1) * count] = picked.T.astype(BF)
    outs = started((picks,), (picks_out,), out_sems)
    moves[1].wait()
    copied = jnp.sum(jnp.where(ids[...] >= n_dev, gates[...], 0.0), axis=0, keepdims=True)
    weigh[...] = jnp.concatenate([gates[...], copied, jnp.zeros((5, t), F32)], axis=0).T
    outs += started((weigh,), (weigh_out,), out_sems.at[pl.ds(1, 1)])
    for move in moves[2:] + outs:
        move.wait()


def product(out, rows_x, rows_g, w_in, w_out):
    cut = w_in.shape[1]
    out[:, :cut] = dot(rows_x, w_in[...]).astype(BF)
    out[:, cut:] = dot_t(rows_g, w_out[...]).astype(BF)


def first_body(n_dev, me, recv, w_in, w_out, partial, rows, wide):
    wide[...] = recv[...].astype(F32)
    width = w_in.shape[0]
    for a in range(2):
        rows[:, a * width : (a + 1) * width] = unpack(wide, a, n_dev, width).astype(BF)
    count = partial.shape[0]
    other = rows_at((1 - place_of(me)[0]) * count, count)
    product(partial, rows[other, :width], rows[other, width:], w_in, w_out)


def own_body(me, rows, w_in, w_out, partial):
    width = w_in.shape[0]
    count = partial.shape[0]
    own = rows_at(place_of(me)[0] * count, count)
    product(partial, rows[own, :width], rows[own, width:], w_in, w_out)


def third_body(me, mine, from_core, to_after, to_before, total):
    chip = place_of(me)[2]
    count = total.shape[0]

    def two(block):
        block = jnp.where(block >= 3, block - 3, block)
        part = rows_at(block * count, count)
        return mine[part, :].astype(F32) + from_core[part, :].astype(F32)

    to_after[...] = two(chip + 1).astype(BF)
    to_before[...] = two(chip + 2).astype(BF)
    total[...] = two(chip)


def half_body(total, from_before, from_after, to_half, total_out):
    value = total[...] + from_before[...].astype(F32) + from_after[...].astype(F32)
    to_half[...] = value.astype(BF)
    total_out[...] = value


def finish_body(total, from_half, block):
    cut = total.shape[1] // 3
    value = total[...] + from_half[...].astype(F32)
    gate_part, up_part, hidden_grad = value[:, :cut], value[:, cut : 2 * cut], value[:, 2 * cut :]
    sig = jax.nn.sigmoid(gate_part)
    silu = gate_part * sig
    dsilu = sig * (1.0 + gate_part * (1.0 - sig))
    block[:, :cut] = (silu * up_part).astype(BF)
    block[:, cut : 2 * cut] = (hidden_grad * up_part * dsilu).astype(BF)
    block[:, 2 * cut :] = (hidden_grad * silu).astype(BF)


def expert_rows(hidden, w_in, w_out):
    half = w_out.shape[0]
    return dot(hidden[:, :half], w_out[...]), dot_t(hidden[:, half:], w_in[...])


def rows_body(hidden, w_in, w_out, tokens_in, grad_in, out, tokens, grad_out, sems):
    moves = started((tokens_in, grad_in), (tokens, grad_out), sems)
    width = w_in.shape[0]
    value, grad = expert_rows(hidden, w_in, w_out)
    out[:, :width] = value
    out[:, width:] = grad
    for move in moves:
        move.wait()


def back_body(n_dev, me, hidden, own_rows, w_in, w_out, send, wide):
    width = w_in.shape[0]
    value, grad = expert_rows(hidden, w_in, w_out)
    core = place_of(me)[0]
    pieces = width // LANES
    stride = 2 * CAP * pieces
    count = hidden.shape[0] // 6
    for c in range(2):
        for i in range(6):
            row = ((core ^ c) * 6 + i) * count
            slot = row // n_dev
            start = (row - slot * n_dev) * stride + slot * pieces
            for a in range(2):
                for q in range(pieces):
                    left = q * LANES
                    if c == 0:
                        left = left + a * width
                        piece = own_rows[i * count : (i + 1) * count, left : left + LANES]
                    else:
                        piece = (value, grad)[a][i * count : (i + 1) * count, left : left + LANES]
                    at = pl.ds(start + a * CAP * pieces + q, count, stride=stride)
                    wide[at, :] = piece
    send[...] = wide[...].astype(BF)


def combine_body(n_dev, recv, picks, weigh, tokens, grad_out, moe_out, grad_tokens, wide):
    t, width = tokens.shape
    wide[...] = recv[...].astype(F32)
    back_out = unpack(wide, 0, n_dev, width).astype(BF)
    back_grad = unpack(wide, 1, n_dev, width).astype(BF)
    count = CAP * n_dev
    take = [picks[:, :count], picks[:, count:]]
    copied = weigh[:, 2:3]
    moe = weigh[:, 0:1] * dot(take[0], back_out) + weigh[:, 1:2] * dot(take[1], back_out)
    moe_out[...] = (moe + copied * tokens[...].astype(F32)).astype(BF)
    grad = dot(take[0] + take[1], back_grad)
    grad_tokens[...] = (grad + copied * grad_out[...].astype(F32)).astype(BF)


def per_device(tokens, grad_out, expert_ids, gates, w_in, w_out):
    n_dev = lax.axis_size("expert")
    n_dp = lax.axis_size("dp")
    t, width = tokens.shape
    half = w_out.shape[1]
    count = n_dev * CAP
    wide_rows = 2 * count * width // LANES
    wide = pltpu.VMEM((wide_rows, LANES), F32)
    shape = jax.ShapeDtypeStruct

    me = lax.axis_index("dp").astype(jnp.int32).reshape(1)
    cores = [(i, i ^ 1) for i in range(n_dp)]
    triples = [[h * 6 + c + 2 * i for i in range(3)] for h in range(2) for c in range(2)]
    halves = [(i, (i + 6) % n_dp) for i in range(n_dp)]
    after = [(i, i // 6 * 6 + (i + 2) % 6) for i in range(n_dp)]
    before = [(i, i // 6 * 6 + (i + 4) % 6) for i in range(n_dp)]

    lines = [pltpu.VMEM((2, t), jnp.int32), pltpu.VMEM((2, t), F32)]
    (send,) = call(
        functools.partial(send_body, n_dev),
        [pltpu.HBM((wide_rows, LANES), BF)],
        [expert_ids.T, gates.T, tokens, grad_out],
        [
            *lines,
            pltpu.VMEM((t, width), BF),
            pltpu.VMEM((t, width), BF),
            pltpu.VMEM((wide_rows, LANES), BF),
            wide,
            pltpu.SemaphoreType.DMA((4,)),
            pltpu.SemaphoreType.DMA((4,)),
        ],
        2 * (2 * count * t * width + n_dev * t * t),
        range(4),
    )
    picks, weigh, *weights = call(
        functools.partial(ready_body, n_dev),
        [
            pltpu.HBM((t, 2 * count), BF),
            pltpu.HBM((t, 8), F32),
            shape(w_in.shape[1:], BF),
            shape(w_out.shape[1:], BF),
        ],
        [expert_ids.T, gates.T, w_in[0], w_out[0]],
        [
            pltpu.VMEM((t, 2 * count), BF),
            pltpu.VMEM((t, 8), F32),
            *lines,
            pltpu.SemaphoreType.DMA((4,)),
            pltpu.SemaphoreType.DMA((2,)),
        ],
        2 * n_dev * t * t,
        range(4),
    )

    def exchange(rows):
        parts = rows.reshape(n_dev, wide_rows // n_dev, LANES)
        parts = lax.all_to_all(parts, "expert", split_axis=0, concat_axis=0, tiled=True)
        return parts.reshape(wide_rows, LANES)

    recv = exchange(send)

    cw = 3 * half
    n_core, n_third = count // 2, count // 6
    flops = 2 * n_core * width * cw
    to_core, rows = call(
        functools.partial(first_body, n_dev),
        [shape((n_core, cw), BF), shape((count, 2 * width), BF)],
        [me, recv, *weights],
        [wide],
        flops,
    )
    from_core = lax.ppermute(to_core, "dp", cores)
    (mine,) = call(own_body, [shape((n_core, cw), BF)], [me, rows, *weights], (), flops)

    third = shape((n_third, cw), BF)
    wide_third = shape((n_third, cw), F32)
    to_after, to_before, total = call(third_body, [third, third, wide_third], [me, mine, from_core])
    from_before = lax.ppermute(to_after, "dp", after)
    from_after = lax.ppermute(to_before, "dp", before)
    to_half, total = call(half_body, [third, wide_third], [total, from_before, from_after])
    from_half = lax.ppermute(to_half, "dp", halves)
    (block,) = call(finish_body, [third], [total, from_half])
    own_half = lax.all_gather(block, "dp", axis=0, tiled=True, axis_index_groups=triples)
    other_half = lax.ppermute(own_half, "dp", cores)

    own_rows, tokens, grad_out = call(
        rows_body,
        [shape((n_core, 2 * width), F32), shape((t, width), BF), shape((t, width), BF)],
        [own_half, *weights, tokens, grad_out],
        [pltpu.SemaphoreType.DMA((2,))],
        flops,
        (3, 4),
    )

    (send_back,) = call(
        functools.partial(back_body, n_dev),
        [shape((wide_rows, LANES), BF)],
        [me, other_half, own_rows, *weights],
        [wide],
        flops,
    )
    recv_back = exchange(send_back)

    moe_out, grad_tokens = call(
        functools.partial(combine_body, n_dev),
        [shape((t, width), BF), shape((t, width), BF)],
        [recv_back, picks, weigh, tokens, grad_out],
        [wide],
        2 * 3 * count * t * width,
    )
    return moe_out, grad_tokens


def solution(mesh):
    in_specs = (
        P("expert", "dp"),
        P("expert", "dp"),
        P("expert", None),
        P("expert", None),
        P("expert", "dp", None),
        P("expert", None, "dp"),
    )
    out_specs = (P("expert", "dp"), P("expert", "dp"))
    return jax.shard_map(
        per_device, mesh=mesh, in_specs=in_specs, out_specs=out_specs, check_vma=False
    )
```
